512 devices in a mesh: row: 32 (over x, z_lo, core), col: 16 (over y, z_hi).
Axes of the slice: x: 4, y: 8, z: 8 (z_hi: 2, z_lo: 4; z = z_hi * 4 + z_lo), core: 2. Of those that a mesh axis runs over, the one named last changes fastest.
Arguments:
- tokens: bfloat16 [512, 16384], P('col', 'row'), may hold values from -6 to 6
- gate_weight: bfloat16 [16384, 26624], P('row', 'col'), may hold values from -0.046875 to 0.046875
- up_weight: bfloat16 [16384, 26624], P('row', 'col'), may hold values from -0.046875 to 0.046875
- down_weight: bfloat16 [26624, 16384], P('col', 'row'), may hold values from -0.0390625 to 0.0390625
- adapter_gate_a: bfloat16 [16384, 64], P('row', 'col'), may hold values from -0.75 to 0.75
- adapter_gate_b: bfloat16 [64, 26624], P('row', 'col'), may hold values from -0.01171875 to 0.01171875
- adapter_up_a: bfloat16 [16384, 64], P('row', 'col'), may hold values from -0.75 to 0.75
- adapter_up_b: bfloat16 [64, 26624], P('row', 'col'), may hold values from -0.01171875 to 0.01171875
Outputs:
- mixed: bfloat16 [512, 16384], P('col', 'row')
The draws below stay inside these ranges and needn't reach their ends.
All inputs are finite; a program needn't handle non-finite values.
Results may differ from the reference program's by a relative error of at most 0.02.
Values may be sent and summed in bfloat16 or wider, within the bound.
A program may use at most 128 MiB of HBM per device.

```python
import jax
import jax.numpy as jnp
from jax import lax

D = 16384
FFW = 26624
RANK = 64
TOKENS = 512
N_COL = 16


def level_of(stream_key, extent, shards, low, high):
    loudness, own = 1.0, jax.random.fold_in(stream_key, 6)
    for dim, parts in shards:
        steps = jnp.exp(jax.random.uniform(jax.random.fold_in(own, dim), (parts,), jnp.float32, low / len(shards), high / len(shards)))
        loudness = loudness * jnp.repeat(steps, extent[dim] // parts).reshape([-1 if axis == dim else 1 for axis in range(len(extent))])
    return loudness


def noise(own_key, dims, deviation, bound, split=(), held_as=jnp.bfloat16):
    array = jax.random.normal(own_key, dims, jnp.float32) * deviation
    if len(split) > 0:
        array = level_of(own_key, dims, split, -0.22, 0.18) * array
    return jnp.clip(array, min=-bound, max=bound).astype(held_as)


def setup_inputs(seed: int = 0) -> dict:
    arg_keys = jax.random.split(jax.random.key(seed), 9)
    tokens = noise(arg_keys[0], (TOKENS, D), 1.0, 6.0, ((0, 16), (1, 32)))
    gate_weight = noise(arg_keys[1], (D, FFW), D ** -0.5, 0.046875, ((0, 32), (1, 16)))
    up_weight = noise(arg_keys[2], (D, FFW), D ** -0.5, 0.046875, ((0, 32), (1, 16)))
    down_weight = noise(arg_keys[3], (FFW, D), FFW ** -0.5, 0.0390625, ((0, 16), (1, 32)))
    adapter_gate_a = noise(arg_keys[4], (D, RANK), RANK ** -0.5, 0.75, ((0, 32), (1, 16)))
    adapter_gate_b = noise(arg_keys[5], (RANK, FFW), (16 * D) ** -0.5, 0.01171875, ((0, 32), (1, 16)))
    adapter_up_a = noise(arg_keys[6], (D, RANK), RANK ** -0.5, 0.75, ((0, 32), (1, 16)))
    adapter_up_b = noise(arg_keys[7], (RANK, FFW), (16 * D) ** -0.5, 0.01171875, ((0, 32), (1, 16)))
    return {"tokens": tokens, "gate_weight": gate_weight, "up_weight": up_weight, "down_weight": down_weight, "adapter_gate_a": adapter_gate_a, "adapter_gate_b": adapter_gate_b, "adapter_up_a": adapter_up_a, "adapter_up_b": adapter_up_b}


adapter_scale = 2.0


def reference(tokens, gate_weight, up_weight, down_weight, adapter_gate_a, adapter_gate_b, adapter_up_a, adapter_up_b):
    block = FFW // N_COL

    def one_block(index, totals):
        start = (index * block).astype(jnp.int32)
        gate_cols = lax.dynamic_slice_in_dim(gate_weight, start, block, 1)
        up_cols = lax.dynamic_slice_in_dim(up_weight, start, block, 1)
        gate_b = lax.dynamic_slice_in_dim(adapter_gate_b, start, block, 1)
        up_b = lax.dynamic_slice_in_dim(adapter_up_b, start, block, 1)
        down_rows = lax.dynamic_slice_in_dim(down_weight, start, block, 0)
        gate_delta = adapter_scale * jnp.dot(adapter_gate_a, gate_b, preferred_element_type=jnp.float32)
        up_delta = adapter_scale * jnp.dot(adapter_up_a, up_b, preferred_element_type=jnp.float32)
        gate_merged = (gate_cols.astype(jnp.float32) + gate_delta).astype(jnp.bfloat16)
        up_merged = (up_cols.astype(jnp.float32) + up_delta).astype(jnp.bfloat16)
        gate = jnp.dot(tokens, gate_merged, preferred_element_type=jnp.float32)
        upper = jnp.dot(tokens, up_merged, preferred_element_type=jnp.float32)
        hidden = (jax.nn.silu(gate) * upper).astype(jnp.bfloat16)
        return totals + jnp.dot(hidden, down_rows, preferred_element_type=jnp.float32)

    totals = lax.fori_loop(0, N_COL, one_block, jnp.zeros((TOKENS, D), jnp.float32))
    return totals.astype(jnp.bfloat16)
```

```python
import jax
import jax.numpy as jnp
from jax import lax
from jax.experimental import pallas as pl
from jax.experimental.pallas import tpu as pltpu
from jax.sharding import PartitionSpec as P

FEAT = 512
UNITS = 1664
RANKS = 128
WIDE = UNITS + RANKS
OUT = 512
MESH = pl.DeviceIdType.MESH
F32 = jnp.float32
BF16 = jnp.bfloat16


def kernel(
    tok_hbm, gw_hbm, uw_hbm, dw_hbm, ag_hbm, bg_hbm, au_hbm, bu_hbm,
    o_ref,
    gw, uw, dw, ag, au, bg, bu,
    tok, first, second, second_flat,
    part, from_core, x1_out, x1_in, x2_out, x2_in, z_out, z_in,
    hid, hid_flat, out_terms, out_in, last_out, last_in,
    local_sem, send_sem, recv_sem,
):
    row, col = lax.axis_index("row"), lax.axis_index("col")
    x, z, core = row // 8, (row // 2) % 4, row % 2
    y, zh = col // 2, col % 2

    def device(x=x, z=z, core=core, y=y, zh=zh):
        return ((x * 4 + z) * 2 + core, y * 2 + zh)

    other = 1 - core
    ring_a = device(x=x + 1 - 2 * (x % 2))
    ring_b = device(x=3 - x)
    bit_b = x // 2
    bit_a = (x % 2 + bit_b) % 2
    far_x = device(x=(x + 2) % 4)
    core_peer = device(core=other)
    zh_peer = device(zh=1 - zh)
    y_peers = [device(y=(y + k) % 8) for k in range(1, 8)]
    z_peers = [device(z=(z + k) % 4) for k in range(1, 4)]

    def fetch(src, dst, n):
        copy = pltpu.make_async_copy(src, dst, local_sem.at[n])
        copy.start()
        return copy

    small = [
        fetch(ag_hbm, ag, 0), fetch(au_hbm, au, 1), fetch(bg_hbm, bg, 2), fetch(bu_hbm, bu, 3),
    ]
    own_tokens = fetch(tok_hbm, tok.at[zh, y], 4)
    weights = [fetch(gw_hbm, gw, 5), fetch(uw_hbm, uw, 6)]
    down = fetch(dw_hbm, dw, 7)

    barrier = pltpu.get_barrier_semaphore()
    partners = [ring_a, ring_b, far_x, core_peer, zh_peer] + y_peers + z_peers
    for peer in partners:
        pl.semaphore_signal(barrier, inc=1, device_id=peer, device_id_type=MESH)

    for copy in small:
        copy.wait()
    a_g, a_u = ag[...].astype(F32), au[...].astype(F32)
    first[col] = jnp.concatenate([a_g[0:2], a_u[0:2], a_g[2:4], a_u[2:4]], 0).astype(BF16)
    b_pair = jnp.concatenate(
        [bg[...].astype(F32), bu[...].astype(F32), jnp.zeros((4, UNITS), F32)], 0
    )
    slot_b = core * 16 + x * 4 + z
    second[slot_b] = b_pair.astype(BF16)
    own_tokens.wait()
    pl.semaphore_wait(barrier, len(partners))

    started = []

    def send(src, dst, peer):
        n = len(started)
        copy = pltpu.make_async_remote_copy(
            src_ref=src, dst_ref=dst, send_sem=send_sem.at[n], recv_sem=recv_sem.at[n],
            device_id=peer, device_id_type=MESH,
        )
        copy.start()
        started.append(copy)
        return copy

    def arrived(copies):
        for copy in copies:
            copy.wait_recv()

    mine, theirs = tok.at[zh, y], tok.at[1 - zh, y]
    a_mine, a_theirs = first.at[col], first.at[y * 2 + 1 - zh]
    zh_in = [send(a_mine, a_mine, zh_peer), send(mine, mine, zh_peer)]
    tok_in = [[], []]
    a_in = []
    for peer in y_peers:
        a_in.append(send(a_mine, a_mine, peer))
    for peer in y_peers:
        tok_in[0].append(send(mine, mine, peer))
    b_in = [send(second.at[slot_b], second.at[slot_b], peer) for peer in z_peers]

    arrived(zh_in)
    for peer in y_peers:
        a_in.append(send(a_theirs, a_theirs, peer))
    for peer in y_peers:
        tok_in[1].append(send(theirs, theirs, peer))
    arrived(b_in)
    b_x = second.at[pl.ds(core * 16 + x * 4, 4)]
    b_in = [send(b_x, b_x, peer) for peer in (ring_a, ring_b, far_x)]

    lane = lax.broadcasted_iota(jnp.int32, (128, RANKS), 1) % 4
    gate_lane = lane < 2

    def project(q, half):
        side = zh if q == 0 else 1 - zh
        x_blk = tok[side, pl.ds(half * 4, 4)].reshape(128, FEAT)

        def paired(g, u):
            pair = jnp.stack([g.reshape(16, 8, 128), u.reshape(16, 8, 128)], 1)
            return pair.reshape(16, 16, 128).astype(BF16)

        def tile(t, carry):
            at = pl.multiple_of(t * 128, 128)
            w = jnp.concatenate([gw[:, pl.ds(at, 128)], uw[:, pl.ds(at, 128)]], 1)
            both = jnp.dot(x_blk, w, preferred_element_type=F32)
            part[q, half, :, :, pl.ds(at, 128)] = paired(both[:, :128], both[:, 128:])
            return carry

        lax.fori_loop(0, UNITS // 128, tile, 0)
        a_all = first[...].astype(F32).reshape(RANKS, FEAT).astype(BF16)
        ranks = lax.dot_general(
            x_blk, a_all, (((1,), (1,)), ((), ())), preferred_element_type=F32
        )
        part[q, half, :, :, UNITS:WIDE] = paired(
            jnp.where(gate_lane, ranks, 0.0), jnp.where(gate_lane, 0.0, ranks)
        )

    def sum_groups(n, terms, dst):
        def group(i, carry):
            total = terms[0](i).astype(F32)
            for term in terms[1:]:
                total = total + term(i).astype(F32)
            dst[i] = total.astype(BF16)
            return carry

        lax.fori_loop(0, n, group, 0)

    split = ((bit_a, bit_b), (bit_b, bit_a))
    first_peer, second_peer = (ring_a, ring_b), (ring_b, ring_a)
    core_in, x1, x2, z_arr, zg, xg1, xg2, core_g = ([None, None] for _ in range(8))
    y_in = [None, None]

    def step_project(q):
        arrived(tok_in[q])
        if q == 0:
            for copy in weights:
                copy.wait()
            arrived(a_in)
        project(q, other)
        core_in[q] = [send(part.at[q, other], from_core.at[q], core_peer)]
        project(q, core)

    def step_x1(q):
        arrived(core_in[q])
        x1[q] = []
        for h in (0, 1):
            base = h * 8 + (1 - split[h][0]) * 4
            sum_groups(
                4,
                [lambda i: part[q, core, base + i], lambda i: from_core[q, base + i]],
                x1_out.at[q, h],
            )
            x1[q].append(send(x1_out.at[q, h], x1_in.at[q, h], first_peer[h]))

    def step_x2(q):
        x2[q] = []
        for h in (0, 1):
            arrived(x1[q][h : h + 1])
            s = 1 - split[h][1]
            base = h * 8 + split[h][0] * 4 + s * 2
            sum_groups(
                2,
                [
                    lambda i: part[q, core, base + i],
                    lambda i: from_core[q, base + i],
                    lambda i: x1_in[q, h, s * 2 + i],
                ],
                x2_out.at[q, h],
            )
            x2[q].append(send(x2_out.at[q, h], x2_in.at[q, h], second_peer[h]))

    def kept_terms(q, k):
        h, low = k // 2, k % 2
        p = jnp.where(h == 0, bit_a, bit_b)
        s = jnp.where(h == 0, bit_b, bit_a)
        base = h * 8 + p * 4 + s * 2 + low
        return (
            part[q, core, base].astype(F32)
            + from_core[q, base].astype(F32)
            + x1_in[q, h, s * 2 + low].astype(F32)
            + x2_in[q, h, low].astype(F32)
        )

    def step_z(q):
        arrived(x2[q])
        z_arr[q] = []
        for k in range(1, 4):
            owner = (z + k) % 4
            z_out[q, k] = kept_terms(q, owner).astype(BF16)
            z_arr[q].append(send(z_out.at[q, k], z_in.at[q, k], z_peers[k - 1]))

    def own_slot():
        h, low = z // 2, z % 2
        p = jnp.where(h == 0, bit_a, bit_b)
        s = jnp.where(h == 0, bit_b, bit_a)
        return h * 8 + p * 4 + s * 2 + low

    def step_hidden(q):
        total = kept_terms(q, z)
        arrived(z_arr[q])
        for k in range(1, 4):
            total = total + z_in[q, k].astype(F32)
        k_at = lax.broadcasted_iota(jnp.int32, (RANKS, 256), 0)
        s_at = lax.broadcasted_iota(jnp.int32, (RANKS, 256), 1)
        r_of = k_at // 4
        meets = ((r_of % 2) * 16 + r_of // 2) * 8 + k_at % 4 == s_at
        spread = jnp.where(meets, 2.0, 0.0).astype(BF16)
        ranks = jnp.dot(
            total[:, UNITS:].astype(BF16), spread, preferred_element_type=F32
        ).astype(BF16)
        both = total[:, :UNITS] + jnp.dot(
            ranks, second_flat[...], preferred_element_type=F32
        )
        gate, up = both[:8], both[8:]
        slot = own_slot()
        hid[q, core, slot] = (gate / (1.0 + jnp.exp(-gate)) * up).astype(BF16)
        ref = hid.at[q, core, slot]
        zg[q] = [send(ref, ref, peer) for peer in z_peers]

    def step_xg1(q):
        arrived(zg[q])
        xg1[q] = []
        for h in (0, 1):
            ref = hid.at[q, core, pl.ds(h * 8 + split[h][0] * 4 + split[h][1] * 2, 2)]
            xg1[q].append(send(ref, ref, second_peer[h]))

    def step_xg2(q):
        xg2[q] = []
        for h in (0, 1):
            arrived(xg1[q][h : h + 1])
            ref = hid.at[q, core, pl.ds(h * 8 + split[h][0] * 4, 4)]
            xg2[q].append(send(ref, ref, first_peer[h]))

    def step_core_g(q):
        arrived(xg2[q])
        ref = hid.at[q, core]
        core_g[q] = [send(ref, ref, core_peer)]

    def down_half(q, half):
        def flat(i, carry):
            two = hid[q, half, pl.ds(i * 2, 2)].astype(F32).reshape(16, UNITS)
            hid_flat[pl.ds(pl.multiple_of(i * 16, 16), 16), :] = two.astype(BF16)
            return carry

        lax.fori_loop(0, 8, flat, 0)
        for n in range(2):
            at = n * 256
            terms = jnp.dot(hid_flat[...], dw[:, at : at + 256], preferred_element_type=F32)
            out_terms[q, pl.ds(half * 4, 4), :, at : at + 256] = terms.astype(BF16).reshape(
                4, 32, 256
            )

    def step_down(q):
        if q == 0:
            down.wait()
        down_half(q, core)
        arrived(core_g[q])
        down_half(q, other)
        y_in[q] = []
        for k in range(1, 8):
            y_in[q].append(
                send(out_terms.at[q, (y + k) % 8], out_in.at[q, k], y_peers[k - 1])
            )

    def y_sum(q):
        arrived(y_in[q])
        total = out_terms[q, y].astype(F32)
        for k in range(1, 8):
            total = total + out_in[q, k].astype(F32)
        return total

    step_project(0)
    step_x1(0)
    arrived(b_in)
    b_core = second.at[pl.ds(core * 16, 16)]
    b_in = [send(b_core, b_core, core_peer)]
    step_project(1)
    step_x2(0)
    step_x1(1)
    arrived(b_in)
    second_flat[...] = second[...].astype(F32).reshape(256, UNITS).astype(BF16)
    step_z(0)
    step_hidden(0)
    step_x2(1)
    step_xg1(0)
    step_z(1)
    step_xg2(0)
    step_hidden(1)
    step_core_g(0)
    step_xg1(1)
    step_down(0)
    step_xg2(1)
    step_core_g(1)
    step_down(1)
    own = y_sum(0)
    last_out[...] = y_sum(1).astype(BF16)
    final = send(last_out, last_in, zh_peer)
    arrived([final])
    o_ref[...] = (own + last_in[...].astype(F32)).astype(BF16)
    for copy in started:
        copy.wait_send()


SENDS = 96


def per_device(tok, gw, uw, dw, ag, bg, au, bu):
    anywhere = pl.BlockSpec(memory_space=pl.ANY)
    v = lambda *shape: pltpu.VMEM(shape, BF16)
    return pl.pallas_call(
        kernel,
        out_shape=jax.ShapeDtypeStruct((32, OUT), BF16),
        in_specs=[anywhere] * 8,
        out_specs=pl.BlockSpec(memory_space=pltpu.VMEM),
        scratch_shapes=[
            v(FEAT, UNITS), v(FEAT, UNITS), v(UNITS, OUT),
            v(4, FEAT), v(4, FEAT), v(2, UNITS), v(2, UNITS),
            v(2, 8, 32, FEAT), v(16, 8, FEAT), v(32, 8, UNITS), v(256, UNITS),
            v(2, 2, 16, 16, WIDE), v(2, 16, 16, WIDE),
            v(2, 2, 4, 16, WIDE), v(2, 2, 4, 16, WIDE),
            v(2, 2, 2, 16, WIDE), v(2, 2, 2, 16, WIDE),
            v(2, 4, 16, WIDE), v(2, 4, 16, WIDE),
            v(2, 2, 16, 8, UNITS), v(128, UNITS),
            v(2, 8, 32, OUT), v(2, 8, 32, OUT), v(32, OUT), v(32, OUT),
            pltpu.SemaphoreType.DMA((8,)),
            pltpu.SemaphoreType.DMA((SENDS,)),
            pltpu.SemaphoreType.DMA((SENDS,)),
        ],
        compiler_params=pltpu.CompilerParams(
            collective_id=0, has_side_effects=True, vmem_limit_bytes=48 * 1024 * 1024
        ),
        name="ffn",
    )(tok, gw, uw, dw, ag.T, bg, au.T, bu)


def solution(mesh):
    weight, down = P("row", "col"), P("col", "row")
    return jax.shard_map(
        per_device,
        mesh=mesh,
        in_specs=(down, weight, weight, down, weight, weight, weight, weight),
        out_specs=down,
        check_vma=False,
    )
```

```python
import jax
import jax.numpy as jnp
from jax import lax
from jax.experimental import pallas as pl
from jax.experimental.pallas import tpu as pltpu
from jax.sharding import PartitionSpec as P

FEAT = 512
UNITS = 1664
RANKS = 128
PART = 896
PARTS = (896, 768)
OUT = 512
MESH = pl.DeviceIdType.MESH
F32 = jnp.float32
BF16 = jnp.bfloat16


def kernel(
    tok_hbm, gw_hbm, uw_hbm, dw_hbm, ag_hbm, bg_hbm, au_hbm, bu_hbm,
    o_ref,
    gw, uw, dw, ag, au, bg, bu,
    tok, first, first_flat, second, second_flat, rank_sums,
    part, from_core, x1_out, x1_in, x2_out, x2_in, z_out, z_in,
    hid, hid_flat, out_terms, y1_in, y2_out, y2_in, y3_in, y4_in, last_out, last_in,
    local_sem, send_sem, recv_sem,
):
    row, col = lax.axis_index("row"), lax.axis_index("col")
    x, z, core = row // 8, (row // 2) % 4, row % 2
    y, zh = col // 2, col % 2

    def device(x=x, z=z, core=core, y=y, zh=zh):
        return ((x * 4 + z) * 2 + core, y * 2 + zh)

    other = 1 - core
    ring_a = device(x=x + 1 - 2 * (x % 2))
    ring_b = device(x=3 - x)
    bit_b = x // 2
    bit_a = (x % 2 + bit_b) % 2
    far_x = device(x=(x + 2) % 4)
    core_peer = device(core=other)
    zh_peer = device(zh=1 - zh)
    y_peer = {k: device(y=(y + k) % 8) for k in (1, -1, 2, -2, 3, -3, 4)}
    z_peers = [device(z=(z + k) % 4) for k in range(1, 4)]

    def fetch(src, dst, n):
        copy = pltpu.make_async_copy(src, dst, local_sem.at[n])
        copy.start()
        return copy

    barrier = pltpu.get_barrier_semaphore()
    partners = [zh_peer, *y_peer.values(), *z_peers, ring_a, ring_b, far_x, core_peer]
    for peer in partners:
        pl.semaphore_signal(barrier, inc=1, device_id=peer, device_id_type=MESH)

    small = [
        fetch(ag_hbm, ag, 0), fetch(au_hbm, au, 1), fetch(bg_hbm, bg, 2), fetch(bu_hbm, bu, 3),
    ]
    own_tokens = fetch(tok_hbm, tok.at[zh, y], 4)
    weights = [fetch(gw_hbm, gw, 5), fetch(uw_hbm, uw, 6)]
    down = fetch(dw_hbm, dw, 7)

    for copy in small:
        copy.wait()
    a_g, a_u = ag[...].astype(F32), au[...].astype(F32)
    first[col] = jnp.concatenate([a_g[0:2], a_u[0:2], a_g[2:4], a_u[2:4]], 0).astype(BF16)
    b_rows = jnp.concatenate([bg[...].astype(F32), bu[...].astype(F32)], 0)
    b_tail = jnp.concatenate([b_rows[:, PART:], jnp.zeros((4, 2 * PART - UNITS), F32)], 1)
    slot_b = core * 16 + x * 4 + z
    second[slot_b] = jnp.concatenate([b_rows[:, :PART], b_tail], 0).astype(BF16)
    pl.semaphore_wait(barrier, len(partners))

    started = []

    def send(src, dst, peer):
        n = len(started)
        copy = pltpu.make_async_remote_copy(
            src_ref=src, dst_ref=dst, send_sem=send_sem.at[n], recv_sem=recv_sem.at[n],
            device_id=peer, device_id_type=MESH,
        )
        copy.start()
        started.append(copy)
        return copy

    def arrived(copies):
        for copy in copies:
            copy.wait_recv()

    def block(side, at):
        return tok.at[side, (y + at) % 8]

    def spread_tokens(side, src):
        return [send(src, block(side, 0), y_peer[k]) for k in (2, -2, 1, -1)]

    def relay_tokens(side, copies):
        arrived(copies[:2])
        low, high = pl.ds(0, 16), pl.ds(16, 16)
        below, above = block(side, -2), block(side, 2)
        return copies[2:] + [
            send(below.at[low], below.at[low], y_peer[2]),
            send(above.at[high], above.at[high], y_peer[-2]),
            send(below, below, y_peer[1]),
            send(above, above, y_peer[-1]),
        ]

    def spread_first(side):
        ref = first.at[y * 2 + side]
        return [send(ref, ref, y_peer[k]) for k in (4, 3, -3, 2, -2, 1, -1)]

    a_zh = [send(first.at[col], first.at[col], zh_peer)]
    tok_zh = [send(tok_hbm, block(zh, 0), zh_peer)]
    tok_in = [spread_tokens(zh, tok_hbm), None]
    a_in = spread_first(zh)
    b_in = [send(second.at[slot_b], second.at[slot_b], peer) for peer in z_peers]

    gate_lane = lax.broadcasted_iota(jnp.int32, (128, RANKS), 1) % 4 < 2

    def project(q, c, half):
        side = zh if q == 0 else 1 - zh
        x_blk = tok[side, pl.ds(half * 4, 4)].reshape(128, FEAT)

        def paired(g, u):
            pair = jnp.stack([g.reshape(16, 8, 128), u.reshape(16, 8, 128)], 1)
            return pair.reshape(16, 16, 128).astype(BF16)

        for at in range(0, PARTS[c], 128):
            w_at = c * PART + at
            w = jnp.concatenate([gw[:, w_at : w_at + 128], uw[:, w_at : w_at + 128]], 1)
            both = jnp.dot(x_blk, w, preferred_element_type=F32)
            part[q, c, half, :, :, at : at + 128] = paired(both[:, :128], both[:, 128:])
        if c == 1:
            ranks = lax.dot_general(
                x_blk, first_flat[...], (((1,), (1,)), ((), ())), preferred_element_type=F32
            )
            part[q, c, half, :, :, PARTS[1] : PART] = paired(
                jnp.where(gate_lane, ranks, 0.0), jnp.where(gate_lane, 0.0, ranks)
            )

    split = ((bit_a, bit_b), (bit_b, bit_a))
    first_peer, second_peer = (ring_a, ring_b), (ring_b, ring_a)
    core_in, x1, x2, z_arr, zg, xg1, xg2, core_g = ({} for _ in range(8))

    def step_project(q, c):
        project(q, c, other)
        core_in[q, c] = send(part.at[q, c, other], from_core.at[q, c], core_peer)
        project(q, c, core)

    def step_x1(q, c):
        arrived([core_in[q, c]])
        x1[q, c] = []
        for h in (0, 1):
            base = h * 8 + (1 - split[h][0]) * 4
            for i in range(4):
                total = part[q, c, core, base + i].astype(F32)
                total = total + from_core[q, c, base + i].astype(F32)
                x1_out[q, c, h, i] = total.astype(BF16)
            x1[q, c].append(send(x1_out.at[q, c, h], x1_in.at[q, c, h], first_peer[h]))

    def step_x2(q, c):
        x2[q, c] = []
        for h in (0, 1):
            arrived(x1[q, c][h : h + 1])
            s = 1 - split[h][1]
            base = h * 8 + split[h][0] * 4 + s * 2
            for i in range(2):
                total = part[q, c, core, base + i].astype(F32)
                total = total + from_core[q, c, base + i].astype(F32)
                total = total + x1_in[q, c, h, s * 2 + i].astype(F32)
                x2_out[q, c, h, i] = total.astype(BF16)
            x2[q, c].append(send(x2_out.at[q, c, h], x2_in.at[q, c, h], second_peer[h]))

    def slot_of(k):
        h, low = k // 2, k % 2
        p = jnp.where(h == 0, bit_a, bit_b)
        s = jnp.where(h == 0, bit_b, bit_a)
        return h, s, low, h * 8 + p * 4 + s * 2 + low

    def kept_terms(q, c, k):
        h, s, low, at = slot_of(k)
        return (
            part[q, c, core, at].astype(F32)
            + from_core[q, c, at].astype(F32)
            + x1_in[q, c, h, s * 2 + low].astype(F32)
            + x2_in[q, c, h, low].astype(F32)
        )

    def step_z(q, c):
        arrived(x2[q, c])
        z_arr[q, c] = []
        for k in (2, 1, 3):
            z_out[q, c, k] = kept_terms(q, c, (z + k) % 4).astype(BF16)
            z_arr[q, c].append(send(z_out.at[q, c, k], z_in.at[q, c, k], z_peers[k - 1]))

    def step_hidden(q, c):
        total = kept_terms(q, c, z)
        arrived(z_arr[q, c])
        for k in range(1, 4):
            total = total + z_in[q, c, k].astype(F32)
        if c == 1:
            k_at = lax.broadcasted_iota(jnp.int32, (RANKS, 256), 0)
            s_at = lax.broadcasted_iota(jnp.int32, (RANKS, 256), 1)
            r_of = k_at // 4
            meets = ((r_of % 2) * 16 + r_of // 2) * 8 + k_at % 4
            ranks = total[:, PARTS[1] :].astype(BF16)
            for n in (0, 1):
                spread = jnp.where(meets + n * 4 == s_at, 2.0, 0.0).astype(BF16)
                rank_sums[q, n] = jnp.dot(
                    ranks, spread, preferred_element_type=F32
                ).astype(BF16)
        both = total[:, : PARTS[c]] + jnp.dot(
            rank_sums[q, c], second_flat[:, : PARTS[c]], preferred_element_type=F32
        )
        gate, up = both[:8], both[8:]
        at = slot_of(z)[3]
        hid[q, c, core, at, :, : PARTS[c]] = (gate / (1.0 + jnp.exp(-gate)) * up).astype(BF16)
        zg[q, c] = [send_hidden(q, c, at, 1, z_peers[k - 1]) for k in (2, 1, 3)]

    def send_hidden(q, c, at, n, peer):
        ref = hid.at[q, c, core, pl.ds(at, n), :, pl.ds(0, PARTS[c])]
        return send(ref, ref, peer)

    def step_xg1(q, c):
        arrived(zg[q, c])
        xg1[q, c] = [
            send_hidden(q, c, h * 8 + split[h][0] * 4 + split[h][1] * 2, 2, second_peer[h])
            for h in (0, 1)
        ]

    def step_xg2(q, c):
        xg2[q, c] = []
        for h in (0, 1):
            arrived(xg1[q, c][h : h + 1])
            xg2[q, c].append(send_hidden(q, c, h * 8 + split[h][0] * 4, 4, first_peer[h]))

    def step_core_g(q, c):
        arrived(xg2[q, c])
        core_g[q, c] = send_hidden(q, c, 0, 16, core_peer)

    def down_half(q, half):
        for c in (0, 1):
            for i in range(0, 16, 2):
                two = hid[q, c, half, i : i + 2, :, : PARTS[c]].astype(F32)
                hid_flat[i * 8 : i * 8 + 16, c * PART : c * PART + PARTS[c]] = two.reshape(
                    16, PARTS[c]
                ).astype(BF16)
        for at in (0, 256):
            terms = jnp.dot(hid_flat[...], dw[:, at : at + 256], preferred_element_type=F32)
            out_terms[q, pl.ds(half * 4, 4), :, at : at + 256] = terms.astype(BF16).reshape(
                4, 32, 256
            )

    y1, y2, y34 = {}, {}, {}

    def step_down(q):
        if q == 0:
            down.wait()
        down_half(q, core)
        arrived([core_g[q, 0], core_g[q, 1]])
        down_half(q, other)

        def terms(k):
            return out_terms.at[q, (y + k) % 8]

        low, high = pl.ds(0, 16), pl.ds(16, 16)
        y34[q] = [
            send(terms(4).at[low], y4_in.at[q, 0], y_peer[2]),
            send(terms(4).at[high], y4_in.at[q, 1], y_peer[-2]),
            send(terms(3), y3_in.at[q, 0], y_peer[1]),
            send(terms(-3), y3_in.at[q, 1], y_peer[-1]),
        ]
        y1[q] = [
            send(terms(1), y1_in.at[q, 0], y_peer[1]),
            send(terms(-1), y1_in.at[q, 1], y_peer[-1]),
        ]

    def step_y2(q):
        arrived(y34[q])
        y2[q] = []
        for n, k in ((0, 2), (1, -2)):
            total = out_terms[q, (y + k) % 8].astype(F32) + y3_in[q, n].astype(F32)
            mine, rest = (total[:16], total[16:]) if n == 0 else (total[16:], total[:16])
            mine = mine + y4_in[q, n].astype(F32)
            y2_out[q, n] = jnp.concatenate(
                [mine, rest] if n == 0 else [rest, mine], 0
            ).astype(BF16)
            y2[q].append(send(y2_out.at[q, n], y2_in.at[q, n], y_peer[k]))

    def y_sum(q):
        arrived(y1[q])
        total = out_terms[q, y].astype(F32)
        total = total + y1_in[q, 0].astype(F32) + y1_in[q, 1].astype(F32)
        arrived(y2[q])
        return total + y2_in[q, 0].astype(F32) + y2_in[q, 1].astype(F32)

    tok_in[0] = relay_tokens(zh, tok_in[0])
    arrived(a_zh)
    a_in = a_in + spread_first(1 - zh)
    arrived(tok_zh)
    tok_in[1] = spread_tokens(1 - zh, block(1 - zh, 0))
    arrived(b_in)
    b_x = second.at[pl.ds(core * 16 + x * 4, 4)]
    b_in = [send(b_x, b_x, peer) for peer in (far_x, ring_a, ring_b)]
    own_tokens.wait()
    weights[0].wait()
    weights[1].wait()
    arrived(tok_in[0])
    step_project(0, 0)
    arrived(a_in)
    first_flat[...] = first[...].astype(F32).reshape(RANKS, FEAT).astype(BF16)
    step_project(0, 1)
    step_x1(0, 0)
    tok_in[1] = relay_tokens(1 - zh, tok_in[1])
    step_x1(0, 1)
    arrived(b_in)
    b_core = second.at[pl.ds(core * 16, 16)]
    b_in = [send(b_core, b_core, core_peer)]
    arrived(tok_in[1])
    step_project(1, 1)
    step_project(1, 0)
    step_x2(0, 0)
    step_x1(1, 1)
    step_x2(0, 1)
    step_x1(1, 0)
    step_z(0, 0)
    arrived(b_in)
    second_flat[...] = second[...].astype(F32).reshape(256, PART).astype(BF16)
    step_x2(1, 1)
    step_z(0, 1)
    step_x2(1, 0)
    step_hidden(0, 1)
    step_hidden(0, 0)
    step_z(1, 1)
    step_xg1(0, 1)
    step_z(1, 0)
    step_xg1(0, 0)
    step_hidden(1, 1)
    step_xg2(0, 1)
    step_hidden(1, 0)
    step_xg2(0, 0)
    step_xg1(1, 1)
    step_core_g(0, 1)
    step_xg1(1, 0)
    step_core_g(0, 0)
    step_xg2(1, 1)
    step_xg2(1, 0)
    step_down(0)
    step_core_g(1, 1)
    step_core_g(1, 0)
    step_y2(0)
    step_down(1)
    own = y_sum(0)
    step_y2(1)
    last_out[...] = y_sum(1).astype(BF16)
    final = send(last_out, last_in, zh_peer)
    arrived([final])
    o_ref[...] = (own + last_in[...].astype(F32)).astype(BF16)
    for copy in started:
        copy.wait_send()


SENDS = 144


def per_device(tok, gw, uw, dw, ag, bg, au, bu):
    in_hbm = pl.BlockSpec(memory_space=pltpu.HBM)
    v = lambda *shape: pltpu.VMEM(shape, BF16)
    return pl.pallas_call(
        kernel,
        out_shape=jax.ShapeDtypeStruct((32, OUT), BF16),
        in_specs=[in_hbm] * 8,
        out_specs=pl.BlockSpec(memory_space=pltpu.VMEM),
        scratch_shapes=[
            v(FEAT, UNITS), v(FEAT, UNITS), v(UNITS, OUT),
            v(4, FEAT), v(4, FEAT), v(2, UNITS), v(2, UNITS),
            v(2, 8, 32, FEAT), v(16, 8, FEAT), v(RANKS, FEAT),
            v(32, 8, PART), v(256, PART), v(2, 2, 16, 256),
            v(2, 2, 2, 16, 16, PART), v(2, 2, 16, 16, PART),
            v(2, 2, 2, 4, 16, PART), v(2, 2, 2, 4, 16, PART),
            v(2, 2, 2, 2, 16, PART), v(2, 2, 2, 2, 16, PART),
            v(2, 2, 4, 16, PART), v(2, 2, 4, 16, PART),
            v(2, 2, 2, 16, 8, PART), v(128, UNITS),
            v(2, 8, 32, OUT), v(2, 2, 32, OUT), v(2, 2, 32, OUT), v(2, 2, 32, OUT),
            v(2, 2, 32, OUT), v(2, 2, 16, OUT), v(32, OUT), v(32, OUT),
            pltpu.SemaphoreType.DMA((8,)),
            pltpu.SemaphoreType.DMA((SENDS,)),
            pltpu.SemaphoreType.DMA((SENDS,)),
        ],
        compiler_params=pltpu.CompilerParams(
            collective_id=0, has_side_effects=True, vmem_limit_bytes=60 * 1024 * 1024
        ),
        name="ffn",
    )(tok, gw, uw, dw, ag.T, bg, au.T, bu)


def solution(mesh):
    weight, down = P("row", "col"), P("col", "row")
    return jax.shard_map(
        per_device,
        mesh=mesh,
        in_specs=(down, weight, weight, down, weight, weight, weight, weight),
        out_specs=down,
        check_vma=False,
    )
```

```python
import jax
import jax.numpy as jnp
from jax import lax
from jax.experimental import pallas as pl
from jax.experimental.pallas import tpu as pltpu
from jax.sharding import PartitionSpec as P

FEAT = 512
UNITS = 1664
RANKS = 128
PART = 896
PARTS = (896, 768)
OUT = 512
MESH = pl.DeviceIdType.MESH
F32 = jnp.float32
BF16 = jnp.bfloat16


def kernel(
    tok_hbm, gw_hbm, uw_hbm, dw_hbm, ag_hbm, bg_hbm, au_hbm, bu_hbm,
    o_ref,
    gw, uw, dw, ag, au, bg, bu,
    tok, first, first_flat, second, second_flat, rank_sums,
    part, from_core, x1_out, x1_in, x2_out, x2_in, z_out, z_in,
    hid, hid_flat, out_terms, y1_in, y2_out, y2_in, y3_in, y4_in, last_out, last_in,
    local_sem, send_sem, recv_sem,
):
    row, col = lax.axis_index("row"), lax.axis_index("col")
    x, z, core = row // 8, (row // 2) % 4, row % 2
    y, zh = col // 2, col % 2

    def device(x=x, z=z, core=core, y=y, zh=zh):
        return ((x * 4 + z) * 2 + core, y * 2 + zh)

    other = 1 - core
    ring_a = device(x=x + 1 - 2 * (x % 2))
    ring_b = device(x=3 - x)
    bit_b = x // 2
    bit_a = (x % 2 + bit_b) % 2
    far_x = device(x=(x + 2) % 4)
    core_peer = device(core=other)
    zh_peer = device(zh=1 - zh)
    y_peer = {k: device(y=(y + k) % 8) for k in (1, -1, 2, -2, 3, -3, 4)}
    z_peers = [device(z=(z + k) % 4) for k in range(1, 4)]

    def fetch(src, dst, n):
        copy = pltpu.make_async_copy(src, dst, local_sem.at[n])
        copy.start()
        return copy

    barrier = pltpu.get_barrier_semaphore()
    partners = [zh_peer, *y_peer.values(), *z_peers, ring_a, ring_b, far_x, core_peer]
    for peer in partners:
        pl.semaphore_signal(barrier, inc=1, device_id=peer, device_id_type=MESH)

    small = [
        fetch(ag_hbm, ag, 0), fetch(au_hbm, au, 1), fetch(bg_hbm, bg, 2), fetch(bu_hbm, bu, 3),
    ]
    own_tokens = fetch(tok_hbm, tok.at[zh, y], 4)
    for copy in small:
        copy.wait()
    a_g, a_u = ag[...].astype(F32), au[...].astype(F32)
    first[col] = jnp.concatenate([a_g[0:2], a_u[0:2], a_g[2:4], a_u[2:4]], 0).astype(BF16)
    b_rows = jnp.concatenate([bg[...].astype(F32), bu[...].astype(F32)], 0)
    b_tail = jnp.concatenate([b_rows[:, PART:], jnp.zeros((4, 2 * PART - UNITS), F32)], 1)
    slot_b = core * 16 + x * 4 + z
    second[slot_b] = jnp.concatenate([b_rows[:, :PART], b_tail], 0).astype(BF16)
    pl.semaphore_wait(barrier, len(partners))

    started = []

    def send(src, dst, peer, start=True):
        n = len(started)
        copy = pltpu.make_async_remote_copy(
            src_ref=src, dst_ref=dst, send_sem=send_sem.at[n], recv_sem=recv_sem.at[n],
            device_id=peer, device_id_type=MESH,
        )
        if start:
            copy.start()
        started.append(copy)
        return copy

    def arrived(copies):
        for copy in copies:
            copy.wait_recv()

    def send_each(n, refs, before=None):
        first_sem = len(started)

        def make(i):
            src, dst, peer = refs(i)
            return pltpu.make_async_remote_copy(
                src_ref=src, dst_ref=dst, send_sem=send_sem.at[first_sem + i],
                recv_sem=recv_sem.at[first_sem + i], device_id=peer, device_id_type=MESH,
            )

        def go(i, carry):
            if before is not None:
                before(i)
            make(i).start()
            return carry

        lax.fori_loop(0, n, go, 0)
        started.extend(make(i) for i in range(n))

        def wait_one(i, carry):
            make(i).wait_recv()
            return carry

        def wait_all():
            lax.fori_loop(0, n, wait_one, 0)

        wait_all.one = lambda i: make(i).wait_recv()
        return wait_all

    def pick(h, a, b):
        if isinstance(h, int):
            return b if h else a
        return jnp.where(h == 0, a, b)

    def block(side, at):
        return tok.at[side, (y + at) % 8]

    def spread_tokens(side, src):
        return [send(src, block(side, 0), y_peer[k]) for k in (2, -2, 1, -1)]

    def relay_tokens(side, copies):
        arrived(copies[:2])
        low, high = pl.ds(0, 16), pl.ds(16, 16)
        below, above = block(side, -2), block(side, 2)
        return copies[2:] + [
            send(below.at[low], below.at[low], y_peer[2]),
            send(above.at[high], above.at[high], y_peer[-2]),
            send(below, below, y_peer[1]),
            send(above, above, y_peer[-1]),
        ]

    def spread_first(side):
        ref = first.at[y * 2 + side]
        return send_each(7, lambda i: (ref, ref, device(y=(y + 1 + i) % 8)))

    a_zh = [send(first.at[col], first.at[col], zh_peer)]
    tok_zh = [send(tok_hbm, block(zh, 0), zh_peer)]
    tok_in = [spread_tokens(zh, tok_hbm), None]
    a_own_in = spread_first(zh)
    b_own = second.at[slot_b]
    b_in = send_each(3, lambda i: (b_own, b_own, device(z=(z + 1 + i) % 4)))

    weights = [fetch(gw_hbm, gw, 5), fetch(uw_hbm, uw, 6)]
    down = fetch(dw_hbm, dw, 7)

    gate_lane = lax.broadcasted_iota(jnp.int32, (128, RANKS), 1) % 4 < 2

    def project(q, c, half):
        side = zh if q == 0 else 1 - zh
        x_blk = tok[side, pl.ds(half * 4, 4)].reshape(128, FEAT)

        def paired(g, u):
            pair = jnp.stack([g.reshape(16, 8, 128), u.reshape(16, 8, 128)], 1)
            return pair.reshape(16, 16, 128).astype(BF16)

        for at in range(0, PARTS[c], 128):
            w_at = c * PART + at
            w = jnp.concatenate([gw[:, w_at : w_at + 128], uw[:, w_at : w_at + 128]], 1)
            both = jnp.dot(x_blk, w, preferred_element_type=F32)
            part[q, c, half, :, :, at : at + 128] = paired(both[:, :128], both[:, 128:])
        if c == 1:
            ranks = lax.dot_general(
                x_blk, first_flat[...], (((1,), (1,)), ((), ())), preferred_element_type=F32
            )
            part[q, c, half, :, :, PARTS[1] : PART] = paired(
                jnp.where(gate_lane, ranks, 0.0), jnp.where(gate_lane, 0.0, ranks)
            )

    x_a, x_b = x + 1 - 2 * (x % 2), 3 - x

    def ring(h):
        return device(x=pick(h, x_a, x_b))

    core_in, x1, x2, z_arr, zg, xg, core_g = ({} for _ in range(7))

    def step_project(q, c):
        core_in[q, c] = send(part.at[q, c, other], from_core.at[q, c], core_peer, start=False)

        def half_step(n, carry):
            project(q, c, pick(n, other, core))

            @pl.when(n == 0)
            def _():
                core_in[q, c].start()

            return carry

        lax.fori_loop(0, 2, half_step, 0)

    def step_x1(q, c):
        arrived([core_in[q, c]])

        def sums(h):
            base = h * 8 + (1 - pick(h, bit_a, bit_b)) * 4

            def group(i, carry):
                total = part[q, c, core, base + i].astype(F32)
                total = total + from_core[q, c, base + i].astype(F32)
                x1_out[q, c, h, i] = total.astype(BF16)
                return carry

            lax.fori_loop(0, 4, group, 0, unroll=2)

        x1[q, c] = send_each(
            2,
            lambda h: (x1_out.at[q, c, h], x1_in.at[q, c, h], ring(h)),
            sums,
        )

    def step_x2(q, c):
        def sums(h):
            x1[q, c].one(h)
            s = 1 - pick(h, bit_b, bit_a)
            base = h * 8 + pick(h, bit_a, bit_b) * 4 + s * 2
            for i in range(2):
                total = part[q, c, core, base + i].astype(F32)
                total = total + from_core[q, c, base + i].astype(F32)
                total = total + x1_in[q, c, h, s * 2 + i].astype(F32)
                x2_out[q, c, h, i] = total.astype(BF16)

        x2[q, c] = send_each(
            2,
            lambda h: (x2_out.at[q, c, h], x2_in.at[q, c, h], ring(1 - h)),
            sums,
        )

    def slot_of(k):
        h, low = k // 2, k % 2
        p = jnp.where(h == 0, bit_a, bit_b)
        s = jnp.where(h == 0, bit_b, bit_a)
        return h, s, low, h * 8 + p * 4 + s * 2 + low

    def kept_terms(q, c, k):
        h, s, low, at = slot_of(k)
        return (
            part[q, c, core, at].astype(F32)
            + from_core[q, c, at].astype(F32)
            + x1_in[q, c, h, s * 2 + low].astype(F32)
            + x2_in[q, c, h, low].astype(F32)
        )

    def step_z(q, c):
        x2[q, c]()

        def sums(i):
            z_out[q, c, i] = kept_terms(q, c, (z + 1 + i) % 4).astype(BF16)

        z_arr[q, c] = send_each(
            3,
            lambda i: (z_out.at[q, c, i], z_in.at[q, c, i], device(z=(z + 1 + i) % 4)),
            sums,
        )

    def step_hidden(q, c):
        total = kept_terms(q, c, z)
        z_arr[q, c]()
        for k in range(3):
            total = total + z_in[q, c, k].astype(F32)
        if c == 1:
            k_at = lax.broadcasted_iota(jnp.int32, (RANKS, 256), 0)
            s_at = lax.broadcasted_iota(jnp.int32, (RANKS, 256), 1)
            r_of = k_at // 4
            meets = ((r_of % 2) * 16 + r_of // 2) * 8 + k_at % 4
            ranks = total[:, PARTS[1] :].astype(BF16)
            for n in (0, 1):
                spread = jnp.where(meets + n * 4 == s_at, 2.0, 0.0).astype(BF16)
                rank_sums[q, n] = jnp.dot(
                    ranks, spread, preferred_element_type=F32
                ).astype(BF16)
        both = total[:, : PARTS[c]] + jnp.dot(
            rank_sums[q, c], second_flat[:, : PARTS[c]], preferred_element_type=F32
        )
        gate, up = both[:8], both[8:]
        at = x * 4 + z
        hid[q, c, core, at, :, : PARTS[c]] = (gate / (1.0 + jnp.exp(-gate)) * up).astype(BF16)
        zg[q, c] = send_hidden(q, c, 3, lambda i: at, 1, lambda i: device(z=(z + 1 + i) % 4))

    def send_hidden(q, c, n, at, groups, peer):
        def refs(i):
            ref = hid.at[q, c, core, pl.ds(at(i), groups), :, pl.ds(0, PARTS[c])]
            return ref, ref, peer(i)

        return send_each(n, refs)

    def step_xg(q, c):
        zg[q, c]()
        xg[q, c] = send_hidden(
            q, c, 3, lambda i: x * 4, 4, lambda i: device(x=(x + 1 + i) % 4)
        )

    def step_core_g(q, c):
        xg[q, c]()
        ref = hid.at[q, c, core, :, :, pl.ds(0, PARTS[c])]
        core_g[q, c] = send(ref, ref, core_peer)

    def down_half(q, half):
        for c in (0, 1):
            for i in range(8):
                h, p, s = i // 4, i // 2 % 2, i % 2
                on_a, on_b = (p, s) if h == 0 else (s, p)
                slot = (2 * on_b + (on_a + on_b) % 2) * 4 + h * 2
                two = hid[q, c, half, slot : slot + 2, :, : PARTS[c]].astype(F32)
                hid_flat[i * 16 : i * 16 + 16, c * PART : c * PART + PARTS[c]] = two.reshape(
                    16, PARTS[c]
                ).astype(BF16)
        for at in (0, 256):
            terms = jnp.dot(hid_flat[...], dw[:, at : at + 256], preferred_element_type=F32)
            out_terms[q, pl.ds(half * 4, 4), :, at : at + 256] = terms.astype(BF16).reshape(
                4, 32, 256
            )

    y1, y2, y34 = {}, {}, {}

    def step_down(q):
        if q == 0:
            down.wait()
        down_half(q, core)
        arrived([core_g[q, 0], core_g[q, 1]])
        down_half(q, other)

        def terms(k):
            return out_terms.at[q, (y + k) % 8]

        low, high = pl.ds(0, 16), pl.ds(16, 16)
        y34[q] = [
            send(terms(4).at[low], y4_in.at[q, 0], y_peer[2]),
            send(terms(4).at[high], y4_in.at[q, 1], y_peer[-2]),
            send(terms(3), y3_in.at[q, 0], y_peer[1]),
            send(terms(-3), y3_in.at[q, 1], y_peer[-1]),
        ]
        y1[q] = [
            send(terms(1), y1_in.at[q, 0], y_peer[1]),
            send(terms(-1), y1_in.at[q, 1], y_peer[-1]),
        ]

    def step_y2(q):
        arrived(y34[q])
        y2[q] = []
        for n, k in ((0, 2), (1, -2)):
            total = out_terms[q, (y + k) % 8].astype(F32) + y3_in[q, n].astype(F32)
            mine, rest = (total[:16], total[16:]) if n == 0 else (total[16:], total[:16])
            mine = mine + y4_in[q, n].astype(F32)
            y2_out[q, n] = jnp.concatenate(
                [mine, rest] if n == 0 else [rest, mine], 0
            ).astype(BF16)
            y2[q].append(send(y2_out.at[q, n], y2_in.at[q, n], y_peer[k]))

    def y_sum(q):
        arrived(y1[q])
        total = out_terms[q, y].astype(F32)
        total = total + y1_in[q, 0].astype(F32) + y1_in[q, 1].astype(F32)
        arrived(y2[q])
        return total + y2_in[q, 0].astype(F32) + y2_in[q, 1].astype(F32)

    tok_in[0] = relay_tokens(zh, tok_in[0])
    arrived(a_zh)
    a_other_in = spread_first(1 - zh)
    arrived(tok_zh)
    tok_in[1] = spread_tokens(1 - zh, block(1 - zh, 0))
    b_in()
    b_x = second.at[pl.ds(core * 16 + x * 4, 4)]
    b_in = send_each(3, lambda i: (b_x, b_x, device(x=(x + 1 + i) % 4)))
    own_tokens.wait()
    weights[0].wait()
    weights[1].wait()
    arrived(tok_in[0])
    step_project(0, 0)
    a_own_in()
    a_other_in()
    first_flat[...] = first[...].astype(F32).reshape(RANKS, FEAT).astype(BF16)
    step_project(0, 1)
    step_x1(0, 0)
    tok_in[1] = relay_tokens(1 - zh, tok_in[1])
    step_x1(0, 1)
    b_in()
    b_core = second.at[pl.ds(core * 16, 16)]
    b_in = [send(b_core, b_core, core_peer)]
    arrived(tok_in[1])
    step_project(1, 1)
    step_project(1, 0)
    step_x2(0, 0)
    step_x1(1, 1)
    step_x2(0, 1)
    step_x1(1, 0)
    step_z(0, 0)
    arrived(b_in)
    second_flat[...] = second[...].astype(F32).reshape(256, PART).astype(BF16)
    step_x2(1, 1)
    step_z(0, 1)
    step_x2(1, 0)
    step_hidden(0, 1)
    step_hidden(0, 0)
    step_z(1, 1)
    step_xg(0, 1)
    step_z(1, 0)
    step_xg(0, 0)
    step_hidden(1, 1)
    step_core_g(0, 1)
    step_hidden(1, 0)
    step_core_g(0, 0)
    step_xg(1, 1)
    step_xg(1, 0)
    step_down(0)
    step_core_g(1, 1)
    step_core_g(1, 0)
    step_y2(0)
    step_down(1)
    own = y_sum(0)
    step_y2(1)
    last_out[...] = y_sum(1).astype(BF16)
    final = send(last_out, last_in, zh_peer)
    arrived([final])
    o_ref[...] = (own + last_in[...].astype(F32)).astype(BF16)
    for copy in started:
        copy.wait_send()


SENDS = 144


def per_device(tok, gw, uw, dw, ag, bg, au, bu):
    in_hbm = pl.BlockSpec(memory_space=pltpu.HBM)
    v = lambda *shape: pltpu.VMEM(shape, BF16)
    return pl.pallas_call(
        kernel,
        out_shape=jax.ShapeDtypeStruct((32, OUT), BF16),
        in_specs=[in_hbm] * 8,
        out_specs=pl.BlockSpec(memory_space=pltpu.VMEM),
        scratch_shapes=[
            v(FEAT, UNITS), v(FEAT, UNITS), v(UNITS, OUT),
            v(4, FEAT), v(4, FEAT), v(2, UNITS), v(2, UNITS),
            v(2, 8, 32, FEAT), v(16, 8, FEAT), v(RANKS, FEAT),
            v(32, 8, PART), v(256, PART), v(2, 2, 16, 256),
            v(2, 2, 2, 16, 16, PART), v(2, 2, 16, 16, PART),
            v(2, 2, 2, 4, 16, PART), v(2, 2, 2, 4, 16, PART),
            v(2, 2, 2, 2, 16, PART), v(2, 2, 2, 2, 16, PART),
            v(2, 2, 4, 16, PART), v(2, 2, 4, 16, PART),
            v(2, 2, 2, 16, 8, PART), v(128, UNITS),
            v(2, 8, 32, OUT), v(2, 2, 32, OUT), v(2, 2, 32, OUT), v(2, 2, 32, OUT),
            v(2, 2, 32, OUT), v(2, 2, 16, OUT), v(32, OUT), v(32, OUT),
            pltpu.SemaphoreType.DMA((8,)),
            pltpu.SemaphoreType.DMA((SENDS,)),
            pltpu.SemaphoreType.DMA((SENDS,)),
        ],
        compiler_params=pltpu.CompilerParams(
            collective_id=0, has_side_effects=True, vmem_limit_bytes=56 * 1024 * 1024
        ),
        name="ffn",
    )(tok, gw, uw, dw, ag.T, bg, au.T, bu)


def solution(mesh):
    weight, down = P("row", "col"), P("col", "row")
    return jax.shard_map(
        per_device,
        mesh=mesh,
        in_specs=(down, weight, weight, down, weight, weight, weight, weight),
        out_specs=down,
        check_vma=False,
    )
```

```python
import jax
import jax.numpy as jnp
from jax import lax
from jax.experimental import pallas as pl
from jax.experimental.pallas import tpu as pltpu
from jax.sharding import PartitionSpec as P

FEAT = 512
UNITS = 1664
RANKS = 128
PART = 896
PARTS = (896, 768)
OUT = 512
MESH = pl.DeviceIdType.MESH
F32 = jnp.float32
BF16 = jnp.bfloat16


def kernel(
    tok_hbm, gw_hbm, uw_hbm, dw_hbm, ag_hbm, bg_hbm, au_hbm, bu_hbm,
    o_ref,
    gw, uw, dw, ag, au, bg, bu,
    tok, first, first_flat, second, second_flat, rank_sums,
    part, from_core, x1_out, x1_in, x2_out, x2_in, z_out, z_in,
    hid, hid_flat, out_terms, y1_in, y2_out, y2_in, y3_in, y4_in, last_out, last_in,
    local_sem, send_sem, recv_sem,
):
    row, col = lax.axis_index("row"), lax.axis_index("col")
    x, z, core = row // 8, (row // 2) % 4, row % 2
    y, zh = col // 2, col % 2

    def device(x=x, z=z, core=core, y=y, zh=zh):
        return ((x * 4 + z) * 2 + core, y * 2 + zh)

    other = 1 - core
    ring_a = device(x=x + 1 - 2 * (x % 2))
    ring_b = device(x=3 - x)
    bit_b = x // 2
    bit_a = (x % 2 + bit_b) % 2
    far_x = device(x=(x + 2) % 4)
    core_peer = device(core=other)
    zh_peer = device(zh=1 - zh)
    y_peer = {k: device(y=(y + k) % 8) for k in (1, -1, 2, -2, 3, -3, 4)}
    z_peers = [device(z=(z + k) % 4) for k in range(1, 4)]

    def fetch(src, dst, n):
        copy = pltpu.make_async_copy(src, dst, local_sem.at[n])
        copy.start()
        return copy

    barrier = pltpu.get_barrier_semaphore()
    partners = [zh_peer, *y_peer.values(), *z_peers, ring_a, ring_b, far_x, core_peer]
    for peer in partners:
        pl.semaphore_signal(barrier, inc=1, device_id=peer, device_id_type=MESH)

    small = [
        fetch(ag_hbm, ag, 0), fetch(au_hbm, au, 1), fetch(bg_hbm, bg, 2), fetch(bu_hbm, bu, 3),
    ]
    own_tokens = fetch(tok_hbm, tok.at[zh, y], 4)
    pl.semaphore_wait(barrier, len(partners))

    started = []

    def send(src, dst, peer, start=True):
        n = len(started)
        copy = pltpu.make_async_remote_copy(
            src_ref=src, dst_ref=dst, send_sem=send_sem.at[n], recv_sem=recv_sem.at[n],
            device_id=peer, device_id_type=MESH,
        )
        if start:
            copy.start()
        started.append(copy)
        return copy

    def arrived(copies):
        for copy in copies:
            copy.wait_recv()

    def send_each(n, refs, before=None):
        first_sem = len(started)

        def make(i):
            src, dst, peer = refs(i)
            return pltpu.make_async_remote_copy(
                src_ref=src, dst_ref=dst, send_sem=send_sem.at[first_sem + i],
                recv_sem=recv_sem.at[first_sem + i], device_id=peer, device_id_type=MESH,
            )

        def go(i, carry):
            if before is not None:
                before(i)
            make(i).start()
            return carry

        lax.fori_loop(0, n, go, 0)
        started.extend(make(i) for i in range(n))

        def wait_one(i, carry):
            make(i).wait_recv()
            return carry

        def wait_all():
            lax.fori_loop(0, n, wait_one, 0)

        wait_all.one = lambda i: make(i).wait_recv()
        return wait_all

    def pick(h, a, b):
        if isinstance(h, int):
            return b if h else a
        return jnp.where(h == 0, a, b)

    def block(side, at):
        return tok.at[side, (y + at) % 8]

    def spread_tokens(side, src):
        return [send(src, block(side, 0), y_peer[k]) for k in (2, -2, 1, -1)]

    def relay_tokens(side, copies):
        arrived(copies[:2])
        low, high = pl.ds(0, 16), pl.ds(16, 16)
        below, above = block(side, -2), block(side, 2)
        return copies[2:] + [
            send(below.at[low], below.at[low], y_peer[2]),
            send(above.at[high], above.at[high], y_peer[-2]),
            send(below, below, y_peer[1]),
            send(above, above, y_peer[-1]),
        ]

    def spread_first(side):
        ref = first.at[y * 2 + side]
        return send_each(7, lambda i: (ref, ref, device(y=(y + 1 + i) % 8)))

    tok_zh = [send(tok_hbm, block(zh, 0), zh_peer)]
    tok_in = [spread_tokens(zh, tok_hbm), None]
    for copy in small:
        copy.wait()
    a_g, a_u = ag[...].astype(F32), au[...].astype(F32)
    first[col] = jnp.concatenate([a_g[0:2], a_u[0:2], a_g[2:4], a_u[2:4]], 0).astype(BF16)
    b_rows = jnp.concatenate([bg[...].astype(F32), bu[...].astype(F32)], 0)
    b_tail = jnp.concatenate([b_rows[:, PART:], jnp.zeros((4, 2 * PART - UNITS), F32)], 1)
    slot_b = core * 16 + x * 4 + z
    second[slot_b] = jnp.concatenate([b_rows[:, :PART], b_tail], 0).astype(BF16)
    a_zh = [send(first.at[col], first.at[col], zh_peer)]
    a_own_in = spread_first(zh)
    b_own = second.at[slot_b]
    b_in = send_each(3, lambda i: (b_own, b_own, device(z=(z + 1 + i) % 4)))

    weights = [fetch(gw_hbm, gw, 5), fetch(uw_hbm, uw, 6)]
    down = fetch(dw_hbm, dw, 7)

    gate_lane = lax.broadcasted_iota(jnp.int32, (128, RANKS), 1) % 4 < 2

    def project(q, c, half):
        side = zh if q == 0 else 1 - zh
        x_blk = tok[side, pl.ds(half * 4, 4)].reshape(128, FEAT)

        def paired(g, u):
            pair = jnp.stack([g.reshape(16, 8, 128), u.reshape(16, 8, 128)], 1)
            return pair.reshape(16, 16, 128).astype(BF16)

        for at in range(0, PARTS[c], 128):
            w_at = c * PART + at
            w = jnp.concatenate([gw[:, w_at : w_at + 128], uw[:, w_at : w_at + 128]], 1)
            both = jnp.dot(x_blk, w, preferred_element_type=F32)
            part[q, c, half, :, :, at : at + 128] = paired(both[:, :128], both[:, 128:])
        if c == 1:
            ranks = lax.dot_general(
                x_blk, first_flat[...], (((1,), (1,)), ((), ())), preferred_element_type=F32
            )
            part[q, c, half, :, :, PARTS[1] : PART] = paired(
                jnp.where(gate_lane, ranks, 0.0), jnp.where(gate_lane, 0.0, ranks)
            )

    x_a, x_b = x + 1 - 2 * (x % 2), 3 - x

    def ring(h):
        return device(x=pick(h, x_a, x_b))

    core_in, x1, x2, z_arr, zg, xg, core_g = ({} for _ in range(7))

    def step_project(q, c):
        core_in[q, c] = send(part.at[q, c, other], from_core.at[q, c], core_peer, start=False)

        def half_step(n, carry):
            project(q, c, pick(n, other, core))

            @pl.when(n == 0)
            def _():
                core_in[q, c].start()

            return carry

        lax.fori_loop(0, 2, half_step, 0)

    def step_x1(q, c):
        arrived([core_in[q, c]])

        def sums(h):
            base = h * 8 + (1 - pick(h, bit_a, bit_b)) * 4

            def group(i, carry):
                total = part[q, c, core, base + i].astype(F32)
                total = total + from_core[q, c, base + i].astype(F32)
                x1_out[q, c, h, i] = total.astype(BF16)
                return carry

            lax.fori_loop(0, 4, group, 0, unroll=2)

        x1[q, c] = send_each(
            2,
            lambda h: (x1_out.at[q, c, h], x1_in.at[q, c, h], ring(h)),
            sums,
        )

    def step_x2(q, c):
        def sums(h):
            x1[q, c].one(h)
            s = 1 - pick(h, bit_b, bit_a)
            base = h * 8 + pick(h, bit_a, bit_b) * 4 + s * 2
            for i in range(2):
                total = part[q, c, core, base + i].astype(F32)
                total = total + from_core[q, c, base + i].astype(F32)
                total = total + x1_in[q, c, h, s * 2 + i].astype(F32)
                x2_out[q, c, h, i] = total.astype(BF16)

        x2[q, c] = send_each(
            2,
            lambda h: (x2_out.at[q, c, h], x2_in.at[q, c, h], ring(1 - h)),
            sums,
        )

    def slot_of(k):
        h, low = k // 2, k % 2
        p = jnp.where(h == 0, bit_a, bit_b)
        s = jnp.where(h == 0, bit_b, bit_a)
        return h, s, low, h * 8 + p * 4 + s * 2 + low

    def kept_terms(q, c, k):
        h, s, low, at = slot_of(k)
        return (
            part[q, c, core, at].astype(F32)
            + from_core[q, c, at].astype(F32)
            + x1_in[q, c, h, s * 2 + low].astype(F32)
            + x2_in[q, c, h, low].astype(F32)
        )

    def step_z(q, c):
        x2[q, c]()

        def sums(i):
            z_out[q, c, i] = kept_terms(q, c, (z + 1 + i) % 4).astype(BF16)

        z_arr[q, c] = send_each(
            3,
            lambda i: (z_out.at[q, c, i], z_in.at[q, c, i], device(z=(z + 1 + i) % 4)),
            sums,
        )

    def step_hidden(q, c):
        total = kept_terms(q, c, z)
        z_arr[q, c]()
        for k in range(3):
            total = total + z_in[q, c, k].astype(F32)
        if c == 1:
            k_at = lax.broadcasted_iota(jnp.int32, (RANKS, 256), 0)
            s_at = lax.broadcasted_iota(jnp.int32, (RANKS, 256), 1)
            r_of = k_at // 4
            meets = ((r_of % 2) * 16 + r_of // 2) * 8 + k_at % 4
            ranks = total[:, PARTS[1] :].astype(BF16)
            for n in (0, 1):
                spread = jnp.where(meets + n * 4 == s_at, 2.0, 0.0).astype(BF16)
                rank_sums[q, n] = jnp.dot(
                    ranks, spread, preferred_element_type=F32
                ).astype(BF16)
        both = total[:, : PARTS[c]] + jnp.dot(
            rank_sums[q, c], second_flat[:, : PARTS[c]], preferred_element_type=F32
        )
        gate, up = both[:8], both[8:]
        at = x * 4 + z
        hid[q, c, core, at, :, : PARTS[c]] = (gate / (1.0 + jnp.exp(-gate)) * up).astype(BF16)
        zg[q, c] = send_hidden(q, c, 3, lambda i: at, 1, lambda i: device(z=(z + 1 + i) % 4))

    def send_hidden(q, c, n, at, groups, peer):
        def refs(i):
            ref = hid.at[q, c, core, pl.ds(at(i), groups), :, pl.ds(0, PARTS[c])]
            return ref, ref, peer(i)

        return send_each(n, refs)

    def step_xg(q, c):
        zg[q, c]()
        xg[q, c] = send_hidden(
            q, c, 3, lambda i: x * 4, 4, lambda i: device(x=(x + 1 + i) % 4)
        )

    def step_core_g(q, c):
        xg[q, c]()
        ref = hid.at[q, c, core, :, :, pl.ds(0, PARTS[c])]
        core_g[q, c] = send(ref, ref, core_peer)

    def down_half(q, half):
        for c in (0, 1):
            for i in range(8):
                h, p, s = i // 4, i // 2 % 2, i % 2
                on_a, on_b = (p, s) if h == 0 else (s, p)
                slot = (2 * on_b + (on_a + on_b) % 2) * 4 + h * 2
                two = hid[q, c, half, slot : slot + 2, :, : PARTS[c]].astype(F32)
                hid_flat[i * 16 : i * 16 + 16, c * PART : c * PART + PARTS[c]] = two.reshape(
                    16, PARTS[c]
                ).astype(BF16)
        for at in (0, 256):
            terms = jnp.dot(hid_flat[...], dw[:, at : at + 256], preferred_element_type=F32)
            out_terms[q, pl.ds(half * 4, 4), :, at : at + 256] = terms.astype(BF16).reshape(
                4, 32, 256
            )

    y1, y2, y34 = {}, {}, {}

    def step_down(q):
        if q == 1:
            down.wait()
        down_half(q, core)
        arrived([core_g[q, 0], core_g[q, 1]])
        down_half(q, other)

        def terms(k):
            return out_terms.at[q, (y + k) % 8]

        low, high = pl.ds(0, 16), pl.ds(16, 16)
        y34[q] = [
            send(terms(4).at[low], y4_in.at[q, 0], y_peer[2]),
            send(terms(4).at[high], y4_in.at[q, 1], y_peer[-2]),
            send(terms(3), y3_in.at[q, 0], y_peer[1]),
            send(terms(-3), y3_in.at[q, 1], y_peer[-1]),
        ]
        y1[q] = [
            send(terms(1), y1_in.at[q, 0], y_peer[1]),
            send(terms(-1), y1_in.at[q, 1], y_peer[-1]),
        ]

    def step_y2(q):
        arrived(y34[q])
        y2[q] = []
        for n, k in ((0, 2), (1, -2)):
            total = out_terms[q, (y + k) % 8].astype(F32) + y3_in[q, n].astype(F32)
            mine, rest = (total[:16], total[16:]) if n == 0 else (total[16:], total[:16])
            mine = mine + y4_in[q, n].astype(F32)
            y2_out[q, n] = jnp.concatenate(
                [mine, rest] if n == 0 else [rest, mine], 0
            ).astype(BF16)
            y2[q].append(send(y2_out.at[q, n], y2_in.at[q, n], y_peer[k]))

    def y_sum(q):
        arrived(y1[q])
        total = out_terms[q, y].astype(F32)
        total = total + y1_in[q, 0].astype(F32) + y1_in[q, 1].astype(F32)
        arrived(y2[q])
        return total + y2_in[q, 0].astype(F32) + y2_in[q, 1].astype(F32)

    tok_in[0] = relay_tokens(zh, tok_in[0])
    arrived(tok_zh)
    tok_in[1] = spread_tokens(1 - zh, block(1 - zh, 0))
    arrived(a_zh)
    a_other_in = spread_first(1 - zh)
    b_in()
    b_x = second.at[pl.ds(core * 16 + x * 4, 4)]
    b_in = send_each(3, lambda i: (b_x, b_x, device(x=(x + 1 + i) % 4)))
    own_tokens.wait()
    weights[0].wait()
    weights[1].wait()
    arrived(tok_in[0])
    step_project(0, 0)
    tok_in[1] = relay_tokens(1 - zh, tok_in[1])
    a_own_in()
    a_other_in()
    first_flat[...] = first[...].astype(F32).reshape(RANKS, FEAT).astype(BF16)
    step_project(0, 1)
    step_x1(0, 1)
    arrived(tok_in[1])
    step_project(1, 1)
    step_project(1, 0)
    b_in()
    b_core = second.at[pl.ds(core * 16, 16)]
    b_in = [send(b_core, b_core, core_peer)]
    step_x1(1, 1)
    step_x2(0, 1)
    step_x1(1, 0)
    step_z(0, 1)
    arrived(b_in)
    second_flat[...] = second[...].astype(F32).reshape(256, PART).astype(BF16)
    step_x2(1, 1)
    step_x1(0, 0)
    step_x2(1, 0)
    step_hidden(0, 1)
    step_z(1, 1)
    step_z(1, 0)
    step_xg(0, 1)
    step_x2(0, 0)
    step_hidden(1, 1)
    step_hidden(1, 0)
    step_z(0, 0)
    step_core_g(0, 1)
    step_xg(1, 1)
    step_xg(1, 0)
    step_hidden(0, 0)
    step_core_g(1, 1)
    step_core_g(1, 0)
    step_xg(0, 0)
    step_down(1)
    step_core_g(0, 0)
    step_y2(1)
    step_down(0)
    last_out[...] = y_sum(1).astype(BF16)
    final = send(last_out, last_in, zh_peer)
    step_y2(0)
    own = y_sum(0)
    arrived([final])
    o_ref[...] = (own + last_in[...].astype(F32)).astype(BF16)
    for copy in started:
        copy.wait_send()


SENDS = 144


def per_device(tok, gw, uw, dw, ag, bg, au, bu):
    in_hbm = pl.BlockSpec(memory_space=pltpu.HBM)
    v = lambda *shape: pltpu.VMEM(shape, BF16)
    return pl.pallas_call(
        kernel,
        out_shape=jax.ShapeDtypeStruct((32, OUT), BF16),
        in_specs=[in_hbm] * 8,
        out_specs=pl.BlockSpec(memory_space=pltpu.VMEM),
        scratch_shapes=[
            v(FEAT, UNITS), v(FEAT, UNITS), v(UNITS, OUT),
            v(4, FEAT), v(4, FEAT), v(2, UNITS), v(2, UNITS),
            v(2, 8, 32, FEAT), v(16, 8, FEAT), v(RANKS, FEAT),
            v(32, 8, PART), v(256, PART), v(2, 2, 16, 256),
            v(2, 2, 2, 16, 16, PART), v(2, 2, 16, 16, PART),
            v(2, 2, 2, 4, 16, PART), v(2, 2, 2, 4, 16, PART),
            v(2, 2, 2, 2, 16, PART), v(2, 2, 2, 2, 16, PART),
            v(2, 2, 4, 16, PART), v(2, 2, 4, 16, PART),
            v(2, 2, 2, 16, 8, PART), v(128, UNITS),
            v(2, 8, 32, OUT), v(2, 2, 32, OUT), v(2, 2, 32, OUT), v(2, 2, 32, OUT),
            v(2, 2, 32, OUT), v(2, 2, 16, OUT), v(32, OUT), v(32, OUT),
            pltpu.SemaphoreType.DMA((8,)),
            pltpu.SemaphoreType.DMA((SENDS,)),
            pltpu.SemaphoreType.DMA((SENDS,)),
        ],
        compiler_params=pltpu.CompilerParams(
            collective_id=0, has_side_effects=True, vmem_limit_bytes=56 * 1024 * 1024
        ),
        name="ffn",
    )(tok, gw, uw, dw, ag.T, bg, au.T, bu)


def solution(mesh):
    weight, down = P("row", "col"), P("col", "row")
    return jax.shard_map(
        per_device,
        mesh=mesh,
        in_specs=(down, weight, weight, down, weight, weight, weight, weight),
        out_specs=down,
        check_vma=False,
    )
```
